32 devices in a mesh: row: 4 (over y, x), col: 8 (over z, core).
Axes of the slice: x: 2, y: 2, z: 4, core: 2. Of those that a mesh axis runs over, the one named last changes fastest.
Arguments:
- inv_hessian: float32 [12288, 12288], P('row', 'col'), as said below
- weights: bfloat16 [24576, 12288], P('row', 'col'), may hold values from -6 to 6
- calib: bfloat16 [128, 12288], replicated, may hold values from -6 to 6
- block: int32 [1], replicated, may hold values from 0 to 47
Outputs:
- updated: float32 [12288, 12288], P('row', 'col')
- pruned: bfloat16 [24576, 12288], P('row', 'col')
The draws below stay inside these ranges and needn't reach their ends.
Inputs may be any that keep to these rules, and one draw needn't show every extreme that they name: `inv_hessian`: symmetric and positive definite.
All inputs are finite; a program needn't handle non-finite values.
Results may differ from the reference program's by a relative error of at most 0.002.
Values may be sent and summed in bfloat16 or wider, within the bound.
A program may use at most 128 MiB of HBM per device.

```python
import math
import jax
import jax.numpy as jnp
from jax import lax

D = 12288
FF = 24576
B = 256
CAL = 128


def draw_inv_hessian(key, part):
    base = jax.random.fold_in(key, 17)
    first, second, third, fourth = jax.random.split(base, 4)
    noise = jax.random.normal(first, (D, D), jnp.float32) * (0.35 / math.sqrt(D))
    spread = (noise + noise.T) * 0.7071067811865476
    factor_count = 2 * (D // B)
    owner = jnp.arange(D) // B
    group = jnp.arange(factor_count) // 2
    inside = owner[:, None] == group[None, :]
    local = jnp.where(inside, jax.random.normal(third, (D, factor_count), jnp.float32), 0.0)
    tails = jax.random.normal(fourth, (D, factor_count), jnp.float32) * 0.2
    factors = local + tails
    correlated = 0.15 * jnp.dot(factors, factors.T, precision=lax.Precision.HIGHEST)
    correlated = 0.5 * (correlated + correlated.T)
    diagonal = jnp.exp(jax.random.uniform(second, (D,), jnp.float32, 0.0, math.log(2.5)))
    return spread + correlated + jnp.diag(diagonal)


def level_of(key, dims, shards, least, high):
    loudness, own = 1.0, jax.random.fold_in(key, 6)
    for position, blocks in shards:
        draws = jnp.exp(jax.random.uniform(jax.random.fold_in(own, position), (blocks,), jnp.float32, least / len(shards), high / len(shards)))
        loudness = loudness * jnp.repeat(draws, dims[position] // blocks).reshape([-1 if axis == position else 1 for axis in range(len(dims))])
    return loudness


def normal_values(key, extent, deviation, limit, shards=(), kind=jnp.bfloat16):
    loudness = level_of(key, extent, shards, -0.22, 0.18) if shards else 1.0
    entries = jax.random.normal(key, extent, jnp.float32) * deviation * loudness
    return jnp.minimum(jnp.maximum(entries, -limit), limit).astype(kind)


def setup_inputs(seed: int = 0) -> dict:
    splits = jax.random.split(jax.random.key(seed), 5)
    inv_hessian = draw_inv_hessian(jax.random.fold_in(splits[4], 71), 0)
    weights = normal_values(splits[1], (FF, D), 1.0, 6.0, ((0, 4), (1, 8)))
    calib = normal_values(splits[2], (CAL, D), 1.0, 6.0)
    block = jax.random.randint(splits[3], (1,), 0, D // B).astype(jnp.int32)
    return dict(inv_hessian=inv_hessian, weights=weights, calib=calib, block=block)


def reference(inv_hessian, weights, calib, block):
    highest = lax.Precision.HIGHEST
    calib_f = calib.astype(jnp.float32)
    left = jnp.dot(calib_f, inv_hessian, precision=highest)
    right = jnp.dot(inv_hessian, calib_f.T, precision=highest)
    inner = jnp.eye(CAL, dtype=jnp.float32) + jnp.dot(left, calib_f.T, precision=highest)
    inner = 0.5 * (inner + inner.T)
    factor = jnp.linalg.cholesky(inner)
    solved = jax.scipy.linalg.cho_solve((factor, True), left)
    updated = inv_hessian - jnp.dot(right, solved, precision=highest)
    start = (block[0] * B).astype(jnp.int32)
    strip = lax.dynamic_slice_in_dim(updated, start, B, 0)
    square = lax.dynamic_slice_in_dim(strip, start, B, 1)
    square = 0.5 * (square + square.T)
    square_factor = jnp.linalg.cholesky(square)
    comp = jax.scipy.linalg.cho_solve((square_factor, True), strip).astype(jnp.bfloat16)
    window = lax.dynamic_slice_in_dim(weights, start, B, 1)
    product = jnp.dot(window.astype(jnp.float32), comp.astype(jnp.float32), preferred_element_type=jnp.float32)
    pruned = (weights.astype(jnp.float32) - product).astype(jnp.bfloat16)
    return (updated, pruned)
```

```python
import functools

import jax
import jax.numpy as jnp
from jax import lax
from jax.experimental import pallas as pl
from jax.experimental.pallas import tpu as pltpu
from jax.sharding import PartitionSpec as P

B = 256
NB = 128
HIGH = lax.Precision.HIGHEST
VMEM_LIMIT = 48 * 1024 * 1024


def params(*semantics):
    return pltpu.CompilerParams(
        dimension_semantics=semantics or None, vmem_limit_bytes=VMEM_LIMIT
    )


def dot(a, b):
    return jnp.dot(a, b, precision=HIGH, preferred_element_type=jnp.float32)


def dot_t(a, b):
    return lax.dot_general(
        a, b, (((1,), (1,)), ((), ())), precision=HIGH, preferred_element_type=jnp.float32
    )


def bf_dot(a, b):
    return jnp.dot(a, b, preferred_element_type=jnp.float32)


def split2(x):
    hi = x.astype(jnp.bfloat16)
    lo = (x - hi.astype(jnp.float32)).astype(jnp.bfloat16)
    return hi, lo


def split3(x):
    hi = x.astype(jnp.bfloat16)
    rest = x - hi.astype(jnp.float32)
    mid = rest.astype(jnp.bfloat16)
    return hi, mid, (rest - mid.astype(jnp.float32)).astype(jnp.bfloat16)


def tile_of(n, most):
    t = most
    while n % t:
        t //= 2
    return t


def left_kernel(calib_ref, h_ref, out_ref):
    @pl.when(pl.program_id(0) == 0)
    def _():
        out_ref[...] = jnp.zeros_like(out_ref)

    c = calib_ref[...]
    hi, mid, lo = split3(h_ref[...])
    out_ref[...] += bf_dot(c, hi) + (bf_dot(c, mid) + bf_dot(c, lo))


def left_call(calib_rows, h):
    cal = calib_rows.shape[0]
    rows, cols = h.shape
    t = tile_of(rows, 512)
    return pl.pallas_call(
        left_kernel,
        grid=(rows // t,),
        in_specs=[
            pl.BlockSpec((cal, t), lambda i: (0, i)),
            pl.BlockSpec((t, cols), lambda i: (i, 0)),
        ],
        out_specs=pl.BlockSpec((cal, cols), lambda i: (0, 0)),
        out_shape=jax.ShapeDtypeStruct((cal, cols), jnp.float32),
        compiler_params=params("arbitrary"),
        cost_estimate=pl.CostEstimate(
            flops=6 * cal * rows * cols, bytes_accessed=4 * rows * cols, transcendentals=0
        ),
        name="left_part",
    )(calib_rows, h)


def inverses(mats):
    n = NB
    ri = lax.broadcasted_iota(jnp.int32, (n, n), 0)
    ci = lax.broadcasted_iota(jnp.int32, (n, n), 1)
    scales, ms = [], []
    for m in mats:
        only = jnp.where(ri == ci, m, 0.0)
        s_row = lax.rsqrt(jnp.sum(only, axis=0, keepdims=True))
        s_col = lax.rsqrt(jnp.sum(only, axis=1, keepdims=True))
        scales.append((s_row, s_col))
        ms.append(m * s_row * s_col)
    rk = lax.broadcasted_iota(jnp.int32, (n, 1), 0)
    ck = lax.broadcasted_iota(jnp.int32, (1, n), 1)
    for k in range(n):
        for i, m in enumerate(ms):
            row = m[k : k + 1, :]
            col = m[:, k : k + 1]
            inv = 1.0 / m[k : k + 1, k : k + 1]
            row = (row + jnp.where(ck == k, 1.0, 0.0)) * inv
            col = col - jnp.where(rk == k, 1.0, 0.0)
            ms[i] = m - col * row
    return [m * a * b for m, (a, b) in zip(ms, scales)]


def block_inverse_kernel(a_ref, out_ref):
    n = NB
    a = a_ref[...]
    a = 0.5 * (a + a.T)
    a11, a21, a22 = a[:n, :n], a[n:, :n], a[n:, n:]
    (p,) = inverses([a11])
    p = 0.5 * (p + p.T)
    w = dot(a21, p)
    (q,) = inverses([a22 - dot_t(w, a21)])
    q = 0.5 * (q + q.T)
    off = -dot(q, w)
    out_ref[:n, :n] = p - dot(w.T, off)
    out_ref[n:, :n] = off
    out_ref[:n, n:] = off.T
    out_ref[n:, n:] = q


def block_inverse(a):
    return pl.pallas_call(
        block_inverse_kernel,
        out_shape=jax.ShapeDtypeStruct(a.shape, jnp.float32),
        compiler_params=params(),
        name="block_inverse",
    )(a)


def small_kernel(inner_ref, lmt_ref, ainv_ref, inv_ref, x_ref, sinv_ref):
    inner = inner_ref[...]
    ri = lax.broadcasted_iota(jnp.int32, inner.shape, 0)
    ci = lax.broadcasted_iota(jnp.int32, inner.shape, 1)
    inner = jnp.where(ri == ci, 1.0, 0.0) + 0.5 * (inner + inner.T)
    lmt = lmt_ref[...]
    x = dot(ainv_ref[...], lmt)
    s = inner - dot(lmt.T, x)
    s = 0.5 * (s + s.T)
    a, b = inverses([inner, s])
    inv_ref[...] = 0.5 * (a + a.T)
    sinv_ref[...] = 0.5 * (b + b.T)
    x_ref[...] = x


def small(inner, lmt, ainv):
    f = jnp.float32
    return pl.pallas_call(
        small_kernel,
        out_shape=(
            jax.ShapeDtypeStruct(inner.shape, f),
            jax.ShapeDtypeStruct(lmt.shape, f),
            jax.ShapeDtypeStruct(inner.shape, f),
        ),
        compiler_params=params(),
        name="small_inverses",
    )(inner, lmt, ainv)


def comp_kernel(hm_ref, left_ref, lmt_ref, ainv_ref, x_ref, sinv_ref, out_ref):
    t = dot(ainv_ref[...], hm_ref[...])
    lm = lmt_ref[...].T
    v = dot(sinv_ref[...], left_ref[...] - dot(lm, t))
    out_ref[...] = (t - dot(x_ref[...], v)).astype(jnp.bfloat16)


def comp_call(hm, left, lmt, ainv, x, sinv):
    cols = hm.shape[1]
    t = tile_of(cols, 512)
    whole = lambda a: pl.BlockSpec(a.shape, lambda i: (0, 0))
    wide = lambda a: pl.BlockSpec((a.shape[0], t), lambda i: (0, i))
    return pl.pallas_call(
        comp_kernel,
        grid=(cols // t,),
        in_specs=[wide(hm), wide(left), whole(lmt), whole(ainv), whole(x), whole(sinv)],
        out_specs=pl.BlockSpec((hm.shape[0], t), lambda i: (0, i)),
        out_shape=jax.ShapeDtypeStruct(hm.shape, jnp.bfloat16),
        compiler_params=params("arbitrary"),
        name="comp",
    )(hm, left, lmt, ainv, x, sinv)


def update_kernel(right_ref, inv_ref, left_ref, h_ref, out_ref, s_ref):
    cal = left_ref.shape[0]

    @pl.when(pl.program_id(0) == 0)
    def _():
        hi, lo = split2(dot(inv_ref[...], left_ref[...]))
        s_ref[0:cal] = hi
        s_ref[cal : 2 * cal] = lo
        s_ref[2 * cal : 3 * cal] = hi

    hi, lo = split2(right_ref[...].T)
    r = jnp.concatenate([hi, hi, lo], axis=1)
    out_ref[...] = h_ref[...] - bf_dot(r, s_ref[...])


def update_call(right, inv, left, h):
    cal = left.shape[0]
    rows, cols = h.shape
    t = tile_of(rows, 512)
    return pl.pallas_call(
        update_kernel,
        grid=(rows // t,),
        in_specs=[
            pl.BlockSpec((cal, t), lambda i: (0, i)),
            pl.BlockSpec(inv.shape, lambda i: (0, 0)),
            pl.BlockSpec(left.shape, lambda i: (0, 0)),
            pl.BlockSpec((t, cols), lambda i: (i, 0)),
        ],
        out_specs=pl.BlockSpec((t, cols), lambda i: (i, 0)),
        out_shape=jax.ShapeDtypeStruct(h.shape, jnp.float32),
        scratch_shapes=[pltpu.VMEM((3 * cal, cols), jnp.bfloat16)],
        compiler_params=params("arbitrary"),
        cost_estimate=pl.CostEstimate(
            flops=6 * cal * rows * cols, bytes_accessed=8 * rows * cols, transcendentals=0
        ),
        name="update",
    )(right, inv, left, h)


def prune_kernel(window_ref, comp_ref, w_ref, out_ref):
    product = bf_dot(window_ref[...], comp_ref[...])
    out_ref[...] = (w_ref[...].astype(jnp.float32) - product).astype(jnp.bfloat16)


def prune_call(window, comp, w):
    rows, cols = w.shape
    t = tile_of(rows, 768)
    return pl.pallas_call(
        prune_kernel,
        grid=(rows // t,),
        in_specs=[
            pl.BlockSpec((t, window.shape[1]), lambda i: (i, 0)),
            pl.BlockSpec(comp.shape, lambda i: (0, 0)),
            pl.BlockSpec((t, cols), lambda i: (i, 0)),
        ],
        out_specs=pl.BlockSpec((t, cols), lambda i: (i, 0)),
        out_shape=jax.ShapeDtypeStruct(w.shape, jnp.bfloat16),
        compiler_params=params("arbitrary"),
        cost_estimate=pl.CostEstimate(
            flops=2 * rows * cols * window.shape[1],
            bytes_accessed=4 * rows * cols,
            transcendentals=0,
        ),
        name="prune",
    )(window, comp, w)


def per_device(h, w, calib, block):
    rows, cols = h.shape
    r = lax.axis_index("row")
    c = lax.axis_index("col")
    start = block[0] * B
    owner_row, owner_col = start // rows, start // cols
    mine_row, mine_col = r == owner_row, c == owner_col
    off_row, off_col = start - owner_row * rows, start - owner_col * cols

    win = lax.dynamic_slice_in_dim(w, off_col, B, 1)
    window = lax.psum(jnp.where(mine_col, win, jnp.zeros_like(win)), "col")

    strip = lax.dynamic_slice_in_dim(h, off_row, B, 0)
    strip = jnp.where(mine_row, strip, 0.0)
    square = lax.dynamic_slice_in_dim(strip, off_col, B, 1)
    square = lax.psum(jnp.where(mine_col, square, 0.0), ("row", "col"))

    calib_rows = lax.dynamic_slice_in_dim(calib, r * rows, rows, 1)
    calib_cols = lax.dynamic_slice_in_dim(calib, c * cols, cols, 1).astype(jnp.float32)
    part = left_call(calib_rows, h)
    both = dot_t(jnp.concatenate([part, strip], axis=0), calib_cols)
    both = lax.psum(both, ("row", "col"))
    cal = part.shape[0]
    inner, lmt = both[:cal], both[cal:]
    left = lax.psum(part, "row")
    hm = lax.psum(strip, "row")

    n = rows // cols
    zero = jnp.zeros_like(left)
    right = jnp.concatenate(
        [jnp.where(c == r * n + j, left, zero) for j in range(n)], axis=1
    )
    right = lax.psum(right, "col")

    ainv = block_inverse(square)
    inv, x, sinv = small(inner, lmt, ainv)
    updated = update_call(right, inv, left, h)
    comp = comp_call(hm, left, lmt, ainv, x, sinv)
    pruned = prune_call(window, comp, w)
    return (updated, pruned)


def solution(mesh):
    return jax.shard_map(
        per_device,
        mesh=mesh,
        in_specs=(P("row", "col"), P("row", "col"), P(), P()),
        out_specs=(P("row", "col"), P("row", "col")),
        check_vma=False,
    )
```

```python
import functools

import jax
import jax.numpy as jnp
from jax import lax
from jax.experimental import pallas as pl
from jax.experimental.pallas import tpu as pltpu
from jax.sharding import PartitionSpec as P

B = 256
NB = 128
HIGH = lax.Precision.HIGHEST
VMEM_LIMIT = 48 * 1024 * 1024


def params(*semantics):
    return pltpu.CompilerParams(
        dimension_semantics=semantics or None, vmem_limit_bytes=VMEM_LIMIT
    )


def dot(a, b):
    return jnp.dot(a, b, precision=HIGH, preferred_element_type=jnp.float32)


def dot_t(a, b):
    return lax.dot_general(
        a, b, (((1,), (1,)), ((), ())), precision=HIGH, preferred_element_type=jnp.float32
    )


def bf_dot(a, b):
    return jnp.dot(a, b, preferred_element_type=jnp.float32)


def split2(x):
    hi = x.astype(jnp.bfloat16)
    lo = (x - hi.astype(jnp.float32)).astype(jnp.bfloat16)
    return hi, lo


def split3(x):
    hi = x.astype(jnp.bfloat16)
    rest = x - hi.astype(jnp.float32)
    mid = rest.astype(jnp.bfloat16)
    return hi, mid, (rest - mid.astype(jnp.float32)).astype(jnp.bfloat16)


def tile_of(n, most):
    t = most
    while n % t:
        t //= 2
    return t


def left_kernel(calib_ref, h_ref, out_ref):
    @pl.when(pl.program_id(0) == 0)
    def _():
        out_ref[...] = jnp.zeros_like(out_ref)

    c = calib_ref[...]
    hi, mid, lo = split3(h_ref[...])
    out_ref[...] += bf_dot(c, hi) + (bf_dot(c, mid) + bf_dot(c, lo))


def left_call(calib_rows, h):
    cal = calib_rows.shape[0]
    rows, cols = h.shape
    t = tile_of(rows, 512)
    return pl.pallas_call(
        left_kernel,
        grid=(rows // t,),
        in_specs=[
            pl.BlockSpec((cal, t), lambda i: (0, i)),
            pl.BlockSpec((t, cols), lambda i: (i, 0)),
        ],
        out_specs=pl.BlockSpec((cal, cols), lambda i: (0, 0)),
        out_shape=jax.ShapeDtypeStruct((cal, cols), jnp.float32),
        compiler_params=params("arbitrary"),
        cost_estimate=pl.CostEstimate(
            flops=6 * cal * rows * cols, bytes_accessed=4 * rows * cols, transcendentals=0
        ),
        name="left_part",
    )(calib_rows, h)


def inverses(mats):
    n = NB
    ri = lax.broadcasted_iota(jnp.int32, (n, n), 0)
    ci = lax.broadcasted_iota(jnp.int32, (n, n), 1)
    scales, ms = [], []
    for m in mats:
        only = jnp.where(ri == ci, m, 0.0)
        s_row = lax.rsqrt(jnp.sum(only, axis=0, keepdims=True))
        s_col = lax.rsqrt(jnp.sum(only, axis=1, keepdims=True))
        scales.append((s_row, s_col))
        ms.append(m * s_row * s_col)
    rk = lax.broadcasted_iota(jnp.int32, (n, 1), 0)
    ck = lax.broadcasted_iota(jnp.int32, (1, n), 1)
    for k in range(n):
        for i, m in enumerate(ms):
            row = m[k : k + 1, :]
            col = m[:, k : k + 1]
            inv = 1.0 / m[k : k + 1, k : k + 1]
            row = (row + jnp.where(ck == k, 1.0, 0.0)) * inv
            col = col - jnp.where(rk == k, 1.0, 0.0)
            ms[i] = m - col * row
    return [m * a * b for m, (a, b) in zip(ms, scales)]


def block_inverse_kernel(a_ref, out_ref):
    n = NB
    a = a_ref[...]
    a = 0.5 * (a + a.T)
    a11, a21, a22 = a[:n, :n], a[n:, :n], a[n:, n:]
    (p,) = inverses([a11])
    p = 0.5 * (p + p.T)
    w = dot(a21, p)
    (q,) = inverses([a22 - dot_t(w, a21)])
    q = 0.5 * (q + q.T)
    off = -dot(q, w)
    out_ref[:n, :n] = p - dot(w.T, off)
    out_ref[n:, :n] = off
    out_ref[:n, n:] = off.T
    out_ref[n:, n:] = q


def block_inverse(a):
    return pl.pallas_call(
        block_inverse_kernel,
        out_shape=jax.ShapeDtypeStruct(a.shape, jnp.float32),
        compiler_params=params(),
        name="block_inverse",
    )(a)


def small_kernel(inner_ref, lmt_ref, ainv_ref, inv_ref, x_ref, sinv_ref):
    inner = inner_ref[...]
    ri = lax.broadcasted_iota(jnp.int32, inner.shape, 0)
    ci = lax.broadcasted_iota(jnp.int32, inner.shape, 1)
    inner = jnp.where(ri == ci, 1.0, 0.0) + 0.5 * (inner + inner.T)
    lmt = lmt_ref[...]
    x = dot(ainv_ref[...], lmt)
    s = inner - dot(lmt.T, x)
    s = 0.5 * (s + s.T)
    a, b = inverses([inner, s])
    inv_ref[...] = 0.5 * (a + a.T)
    sinv_ref[...] = 0.5 * (b + b.T)
    x_ref[...] = x


def small(inner, lmt, ainv):
    f = jnp.float32
    return pl.pallas_call(
        small_kernel,
        out_shape=(
            jax.ShapeDtypeStruct(inner.shape, f),
            jax.ShapeDtypeStruct(lmt.shape, f),
            jax.ShapeDtypeStruct(inner.shape, f),
        ),
        compiler_params=params(),
        name="small_inverses",
    )(inner, lmt, ainv)


def comp_kernel(hm_ref, left_ref, lmt_ref, ainv_ref, x_ref, sinv_ref, out_ref):
    t = dot(ainv_ref[...], hm_ref[...])
    lm = lmt_ref[...].T
    v = dot(sinv_ref[...], left_ref[...] - dot(lm, t))
    out_ref[...] = (t - dot(x_ref[...], v)).astype(jnp.bfloat16)


def comp_call(hm, left, lmt, ainv, x, sinv):
    cols = hm.shape[1]
    t = tile_of(cols, 512)
    whole = lambda a: pl.BlockSpec(a.shape, lambda i: (0, 0))
    wide = lambda a: pl.BlockSpec((a.shape[0], t), lambda i: (0, i))
    return pl.pallas_call(
        comp_kernel,
        grid=(cols // t,),
        in_specs=[wide(hm), wide(left), whole(lmt), whole(ainv), whole(x), whole(sinv)],
        out_specs=pl.BlockSpec((hm.shape[0], t), lambda i: (0, i)),
        out_shape=jax.ShapeDtypeStruct(hm.shape, jnp.bfloat16),
        compiler_params=params("arbitrary"),
        name="comp",
    )(hm, left, lmt, ainv, x, sinv)


def exchange_kernel(
    nr, nc, n, g_ref, part_ref, gout, left, right, gbuf, gsum, gbuf2, lbuf,
    g1s, g1r, g2s, g2r, g3s, g3r, l1s, l1r, l2s, l2r, cs, cr, ss, sr,
):
    r = lax.axis_index("row")
    c = lax.axis_index("col")
    grp, lane, ng = c // n, c % n, nc // n
    ch = g_ref.shape[0] // nc
    cal = part_ref.shape[0]
    lc = cal // nr

    def send(src, dst, s, v, axis, peer):
        return pltpu.make_async_remote_copy(
            src_ref=src, dst_ref=dst, send_sem=s, recv_sem=v,
            device_id={axis: peer}, device_id_type=pl.DeviceIdType.MESH,
        )

    def row_peer(d):
        return lax.rem(r + d, nr)

    def col_peer(d):
        return lax.rem(c + d, nc)

    barrier = pltpu.get_barrier_semaphore()
    for d in range(1, nr):
        pl.semaphore_signal(
            barrier, inc=1, device_id={"row": row_peer(d)}, device_id_type=pl.DeviceIdType.MESH
        )
    for d in range(1, nc):
        pl.semaphore_signal(
            barrier, inc=1, device_id={"col": col_peer(d)}, device_id_type=pl.DeviceIdType.MESH
        )
    pl.semaphore_wait(barrier, nr + nc - 2)

    def part_rows(ref, i, size, base=0):
        return ref.at[pl.ds(pl.multiple_of(base + i * size, 8), size)]

    l1, l2, g1, g2, g3 = [], [], [], [], []
    for d in range(1, nr):
        p = row_peer(d)
        l1.append(send(part_rows(part_ref, p, lc), lbuf.at[d], l1s.at[d], l1r.at[d], "row", p))
        l1[-1].start()
    for d in range(1, nc):
        p = col_peer(d)
        g1.append(send(part_rows(g_ref, p, ch), gbuf.at[d], g1s.at[d], g1r.at[d], "col", p))
        g1[-1].start()

    for x in g1:
        x.wait_recv()
    total = g_ref[pl.ds(pl.multiple_of(c * ch, 8), ch)]
    for d in range(1, nc):
        total += gbuf[d]
    gsum[...] = total
    for d in range(1, nr):
        g2.append(send(gsum, gbuf2.at[d], g2s.at[d], g2r.at[d], "row", row_peer(d)))
        g2[-1].start()

    for x in l1:
        x.wait_recv()
    mine = pl.ds(pl.multiple_of(r * lc, 8), lc)
    total = part_ref[mine]
    for d in range(1, nr):
        total += lbuf[d]
    left[mine] = total
    own = part_rows(left, r, lc)
    for d in range(1, nr):
        l2.append(send(own, own, l2s.at[d], l2r.at[d], "row", row_peer(d)))
        l2[-1].start()

    for x in g2:
        x.wait_recv()
    total = gsum[...]
    for d in range(1, nr):
        total += gbuf2[d]
    gout[pl.ds(pl.multiple_of(c * ch, 8), ch)] = total
    gown = part_rows(gout, c, ch)
    for d in range(1, nc):
        g3.append(send(gown, gown, g3s.at[d], g3r.at[d], "col", col_peer(d)))
        g3[-1].start()

    up, down = lax.rem(c + n, nc), lax.rem(c + nc - n, nc)
    origin = grp == r
    to_up = jnp.logical_and(grp >= r, grp + 1 < ng)
    to_down = jnp.logical_and(grp <= r, grp > 0)

    def sibling(e):
        return grp * n + lax.rem(lane + e, n)

    sends = []
    for d in range(nr):
        chunk = lax.rem(r + nr - d, nr)
        src_left = part_rows(left, chunk, lc)
        there = part_rows(right, chunk, lc, lane * cal)

        if d > 0:
            pl.when(origin)(l2[d - 1].wait_recv)

        @pl.when(origin)
        def _():
            rows_in = pl.ds(pl.multiple_of(chunk * lc, 8), lc)
            rows_out = pl.ds(pl.multiple_of(lane * cal + chunk * lc, 8), lc)
            right[rows_out] = left[rows_in]

        u = send(there, there, cs.at[0, d], cr.at[d], "col", up)
        w = send(there, there, cs.at[1, d], cr.at[d], "col", down)
        pl.when(jnp.logical_not(origin))(u.wait_recv)
        pl.when(to_up)(u.start)
        pl.when(to_down)(w.start)
        sends += [(to_up, u), (to_down, w)]
        for e in range(1, n):
            x = send(there, there, ss.at[e, d], sr.at[e, d], "col", sibling(e))
            x.start()
            sends.append((None, x))

    for x in l2:
        pl.when(jnp.logical_not(origin))(x.wait_recv)
    for x in g3:
        x.wait_recv()
    for pred, x in sends:
        if pred is None:
            x.wait()
        else:
            pl.when(pred)(x.wait_send)
    for x in l1 + l2 + g1 + g2 + g3:
        x.wait_send()


def exchange(nr, nc, n, g, part):
    f = jnp.float32
    dma = lambda *shape: pltpu.SemaphoreType.DMA(shape)
    cal, cols = part.shape
    ch = g.shape[0] // nc
    vmem = pl.BlockSpec(memory_space=pltpu.VMEM)
    return pl.pallas_call(
        functools.partial(exchange_kernel, nr, nc, n),
        in_specs=[vmem, vmem],
        out_specs=[vmem, vmem, vmem],
        out_shape=(
            jax.ShapeDtypeStruct(g.shape, f),
            jax.ShapeDtypeStruct(part.shape, f),
            jax.ShapeDtypeStruct((n * cal, cols), f),
        ),
        scratch_shapes=[
            pltpu.VMEM((nc, ch, g.shape[1]), f),
            pltpu.VMEM((ch, g.shape[1]), f),
            pltpu.VMEM((nr, ch, g.shape[1]), f),
            pltpu.VMEM((nr, cal // nr, cols), f),
            dma(nc), dma(nc), dma(nr), dma(nr), dma(nc), dma(nc),
            dma(nr), dma(nr), dma(nr), dma(nr),
            dma(2, nr), dma(nr), dma(n, nr), dma(n, nr),
        ],
        compiler_params=pltpu.CompilerParams(
            collective_id=0, has_side_effects=True, vmem_limit_bytes=VMEM_LIMIT
        ),
        name="exchange",
    )(g, part)


def update_kernel(right_ref, inv_ref, left_ref, h_ref, out_ref, s_ref):
    cal = left_ref.shape[0]

    @pl.when(pl.program_id(0) == 0)
    def _():
        hi, lo = split2(dot(inv_ref[...], left_ref[...]))
        s_ref[0:cal] = hi
        s_ref[cal : 2 * cal] = lo
        s_ref[2 * cal : 3 * cal] = hi

    hi, lo = split2(right_ref[...].T)
    r = jnp.concatenate([hi, hi, lo], axis=1)
    out_ref[...] = h_ref[...] - bf_dot(r, s_ref[...])


def update_call(right, inv, left, h):
    cal = left.shape[0]
    rows, cols = h.shape
    t = tile_of(cols, 512)
    per = cols // t
    return pl.pallas_call(
        update_kernel,
        grid=(rows // t,),
        in_specs=[
            pl.BlockSpec((cal, t), lambda i: (i // per, i % per)),
            pl.BlockSpec(inv.shape, lambda i: (0, 0)),
            pl.BlockSpec(left.shape, lambda i: (0, 0)),
            pl.BlockSpec((t, cols), lambda i: (i, 0)),
        ],
        out_specs=pl.BlockSpec((t, cols), lambda i: (i, 0)),
        out_shape=jax.ShapeDtypeStruct(h.shape, jnp.float32),
        scratch_shapes=[pltpu.VMEM((3 * cal, cols), jnp.bfloat16)],
        compiler_params=params("arbitrary"),
        cost_estimate=pl.CostEstimate(
            flops=6 * cal * rows * cols, bytes_accessed=8 * rows * cols, transcendentals=0
        ),
        name="update",
    )(right, inv, left, h)


def prune_kernel(window_ref, comp_ref, w_ref, out_ref):
    product = bf_dot(window_ref[...], comp_ref[...])
    out_ref[...] = (w_ref[...].astype(jnp.float32) - product).astype(jnp.bfloat16)


def prune_call(window, comp, w):
    rows, cols = w.shape
    t = tile_of(rows, 768)
    return pl.pallas_call(
        prune_kernel,
        grid=(rows // t,),
        in_specs=[
            pl.BlockSpec((t, window.shape[1]), lambda i: (i, 0)),
            pl.BlockSpec(comp.shape, lambda i: (0, 0)),
            pl.BlockSpec((t, cols), lambda i: (i, 0)),
        ],
        out_specs=pl.BlockSpec((t, cols), lambda i: (i, 0)),
        out_shape=jax.ShapeDtypeStruct(w.shape, jnp.bfloat16),
        compiler_params=params("arbitrary"),
        cost_estimate=pl.CostEstimate(
            flops=2 * rows * cols * window.shape[1],
            bytes_accessed=4 * rows * cols,
            transcendentals=0,
        ),
        name="prune",
    )(window, comp, w)


def per_device(h, w, calib, block):
    rows, cols = h.shape
    r = lax.axis_index("row")
    c = lax.axis_index("col")
    start = block[0] * B
    owner_row, owner_col = start // rows, start // cols
    mine_row, mine_col = r == owner_row, c == owner_col
    off_row, off_col = start - owner_row * rows, start - owner_col * cols

    win = lax.dynamic_slice_in_dim(w, off_col, B, 1)
    window = lax.psum(jnp.where(mine_col, win, jnp.zeros_like(win)), "col")

    strip = lax.dynamic_slice_in_dim(h, off_row, B, 0)
    strip = jnp.where(mine_row, strip, 0.0)
    square = lax.dynamic_slice_in_dim(strip, off_col, B, 1)
    square = jnp.where(mine_col, square, 0.0)

    calib_rows = lax.dynamic_slice_in_dim(calib, r * rows, rows, 1)
    calib_cols = lax.dynamic_slice_in_dim(calib, c * cols, cols, 1).astype(jnp.float32)
    part = left_call(calib_rows, h)
    cal = part.shape[0]
    both = dot_t(jnp.concatenate([part, strip], axis=0), calib_cols)
    g = jnp.concatenate([both, square[:, :NB], square[:, NB:]], axis=0)

    g, left, right = exchange(lax.axis_size("row"), lax.axis_size("col"), rows // cols, g, part)
    inner, lmt = g[:cal], g[cal : cal + B]
    square = jnp.concatenate([g[cal + B : cal + 2 * B], g[cal + 2 * B :]], axis=1)

    ainv = block_inverse(square)
    inv, x, sinv = small(inner, lmt, ainv)
    comp = comp_call(strip, left, lmt, ainv, x, sinv)
    comp = lax.psum(jnp.where(mine_row, comp, jnp.zeros_like(comp)), "row")
    updated = update_call(right, inv, left, h)
    pruned = prune_call(window, comp, w)
    return (updated, pruned)


def solution(mesh):
    return jax.shard_map(
        per_device,
        mesh=mesh,
        in_specs=(P("row", "col"), P("row", "col"), P(), P()),
        out_specs=(P("row", "col"), P("row", "col")),
        check_vma=False,
    )
```

```python
import functools

import jax
import jax.numpy as jnp
from jax import lax
from jax.experimental import pallas as pl
from jax.experimental.pallas import tpu as pltpu
from jax.sharding import PartitionSpec as P

B = 256
NB = 128
STEP = 32
HIGH = lax.Precision.HIGHEST
VMEM_LIMIT = 48 * 1024 * 1024


def params(*semantics):
    return pltpu.CompilerParams(
        dimension_semantics=semantics or None, vmem_limit_bytes=VMEM_LIMIT
    )


def dot(a, b):
    return jnp.dot(a, b, precision=HIGH, preferred_element_type=jnp.float32)


def dot_t(a, b):
    return lax.dot_general(
        a, b, (((1,), (1,)), ((), ())), precision=HIGH, preferred_element_type=jnp.float32
    )


def bf_dot(a, b):
    return jnp.dot(a, b, preferred_element_type=jnp.float32)


def split2(x):
    hi = x.astype(jnp.bfloat16)
    lo = (x - hi.astype(jnp.float32)).astype(jnp.bfloat16)
    return hi, lo


def tile_of(n, most):
    t = most
    while n % t:
        t //= 2
    return t


def left_kernel(calib_ref, h_ref, out_ref):
    @pl.when(pl.program_id(0) == 0)
    def _():
        out_ref[...] = jnp.zeros_like(out_ref)

    c = calib_ref[...]
    hi, lo = split2(h_ref[...])
    out_ref[...] += bf_dot(c, hi) + bf_dot(c, lo)


def left_call(calib_rows, h):
    cal = calib_rows.shape[0]
    rows, cols = h.shape
    t = tile_of(rows, 512)
    return pl.pallas_call(
        left_kernel,
        grid=(rows // t,),
        in_specs=[
            pl.BlockSpec((cal, t), lambda i: (0, i)),
            pl.BlockSpec((t, cols), lambda i: (i, 0)),
        ],
        out_specs=pl.BlockSpec((cal, cols), lambda i: (0, 0)),
        out_shape=jax.ShapeDtypeStruct((cal, cols), jnp.float32),
        compiler_params=params("arbitrary"),
        cost_estimate=pl.CostEstimate(
            flops=4 * cal * rows * cols, bytes_accessed=4 * rows * cols, transcendentals=0
        ),
        name="left_part",
    )(calib_rows, h)


def inverses(mats, out):
    n = NB
    ri = lax.broadcasted_iota(jnp.int32, (n, n), 0)
    ci = lax.broadcasted_iota(jnp.int32, (n, n), 1)
    scales, ms = [], []
    for m in mats:
        only = jnp.where(ri == ci, m, 0.0)
        s_row = lax.rsqrt(jnp.sum(only, axis=0, keepdims=True))
        s_col = lax.rsqrt(jnp.sum(only, axis=1, keepdims=True))
        scales.append((s_row, s_col))
        ms.append(m * s_row * s_col)
    rk = lax.broadcasted_iota(jnp.int32, (n, 1), 0)
    ck = lax.broadcasted_iota(jnp.int32, (1, n), 1)
    for k in range(n):
        for i, m in enumerate(ms):
            row = m[k : k + 1, :]
            col = m[:, k : k + 1]
            inv = 1.0 / m[k : k + 1, k : k + 1]
            row = (row + jnp.where(ck == k, 1.0, 0.0)) * inv
            col = col - jnp.where(rk == k, 1.0, 0.0)
            ms[i] = m - col * row
        if k % STEP == STEP - 1:
            yield
    for m, (a, b) in zip(ms, scales):
        m = m * a * b
        out.append(0.5 * (m + m.T))


def small_work(g_ref, ainv_ref, inv_ref, x_ref, sinv_ref):
    n = NB
    cal = inv_ref.shape[0]
    inner = g_ref[0:cal]
    ri = lax.broadcasted_iota(jnp.int32, inner.shape, 0)
    ci = lax.broadcasted_iota(jnp.int32, inner.shape, 1)
    inner = jnp.where(ri == ci, 1.0, 0.0) + 0.5 * (inner + inner.T)
    base = cal + 2 * n
    a11 = g_ref[base : base + n]
    a21 = 0.5 * (g_ref[base + n : base + 2 * n] + g_ref[base + 2 * n : base + 3 * n].T)
    a22 = g_ref[base + 3 * n : base + 4 * n]
    out = []
    yield from inverses([0.5 * (a11 + a11.T)], out)
    p = out[0]
    w = dot(a21, p)
    q = 0.5 * (a22 + a22.T) - dot_t(w, a21)
    out = []
    yield from inverses([0.5 * (q + q.T), inner], out)
    q, inv = out
    inv_ref[...] = inv
    off = -dot(q, w)
    ainv_ref[:n, :n] = p - dot(w.T, off)
    ainv_ref[n:, :n] = off
    ainv_ref[:n, n:] = off.T
    ainv_ref[n:, n:] = q
    lmt = g_ref[cal:base]
    x = dot(ainv_ref[...], lmt)
    x_ref[...] = x
    sq = inner - dot(lmt.T, x)
    out = []
    yield from inverses([0.5 * (sq + sq.T)], out)
    sinv_ref[...] = out[0]


def comp_kernel(hm_ref, left_ref, lmt_ref, ainv_ref, x_ref, sinv_ref, out_ref):
    t = dot(ainv_ref[...], hm_ref[...])
    lm = lmt_ref[...].T
    v = dot(sinv_ref[...], left_ref[...] - dot(lm, t))
    out_ref[...] = (t - dot(x_ref[...], v)).astype(jnp.bfloat16)


def comp_call(hm, left, lmt, ainv, x, sinv):
    cols = hm.shape[1]
    t = tile_of(cols, 512)
    whole = lambda a: pl.BlockSpec(a.shape, lambda i: (0, 0))
    wide = lambda a: pl.BlockSpec((a.shape[0], t), lambda i: (0, i))
    return pl.pallas_call(
        comp_kernel,
        grid=(cols // t,),
        in_specs=[wide(hm), wide(left), whole(lmt), whole(ainv), whole(x), whole(sinv)],
        out_specs=pl.BlockSpec((hm.shape[0], t), lambda i: (0, i)),
        out_shape=jax.ShapeDtypeStruct(hm.shape, jnp.bfloat16),
        compiler_params=params("arbitrary"),
        name="comp",
    )(hm, left, lmt, ainv, x, sinv)


def exchange_kernel(
    nr, nc, n, g_ref, part_ref, strip_ref, gout, left, right, hm, ainv, inv, x_out, sinv,
    gbuf, gsum, gbuf2, lbuf, hbuf,
    g1s, g1r, g2s, g2r, g3s, g3r, l1s, l1r, l2s, l2r, cs, cr, ss, sr, h1s, h1r, h2s, h2r,
):
    r = lax.axis_index("row")
    c = lax.axis_index("col")
    grp, lane, ng = c // n, c % n, nc // n
    ch = g_ref.shape[0] // nc
    cal = part_ref.shape[0]
    lc = cal // nr
    hc = strip_ref.shape[0] // nr

    def send(src, dst, s, v, axis, peer):
        return pltpu.make_async_remote_copy(
            src_ref=src, dst_ref=dst, send_sem=s, recv_sem=v,
            device_id={axis: peer}, device_id_type=pl.DeviceIdType.MESH,
        )

    def row_peer(d):
        return lax.rem(r + d, nr)

    def col_peer(d):
        return lax.rem(c + d, nc)

    barrier = pltpu.get_barrier_semaphore()
    for d in range(1, nr):
        pl.semaphore_signal(
            barrier, inc=1, device_id={"row": row_peer(d)}, device_id_type=pl.DeviceIdType.MESH
        )
    for d in range(1, nc):
        pl.semaphore_signal(
            barrier, inc=1, device_id={"col": col_peer(d)}, device_id_type=pl.DeviceIdType.MESH
        )
    pl.semaphore_wait(barrier, nr + nc - 2)

    def part_rows(ref, i, size, base=0):
        return ref.at[pl.ds(pl.multiple_of(base + i * size, 8), size)]

    l1, l2, g1, g2, g3, h1, h2 = [], [], [], [], [], [], []
    for d in range(1, nr):
        p = row_peer(d)
        l1.append(send(part_rows(part_ref, p, lc), lbuf.at[d], l1s.at[d], l1r.at[d], "row", p))
        l1[-1].start()
    for d in range(1, nc):
        p = col_peer(d)
        g1.append(send(part_rows(g_ref, p, ch), gbuf.at[d], g1s.at[d], g1r.at[d], "col", p))
        g1[-1].start()
    for d in range(1, nr):
        p = row_peer(d)
        h1.append(send(part_rows(strip_ref, p, hc), hbuf.at[d], h1s.at[d], h1r.at[d], "row", p))
        h1[-1].start()

    for x in g1:
        x.wait_recv()
    total = g_ref[pl.ds(pl.multiple_of(c * ch, 8), ch)]
    for d in range(1, nc):
        total += gbuf[d]
    gsum[...] = total
    for d in range(1, nr):
        g2.append(send(gsum, gbuf2.at[d], g2s.at[d], g2r.at[d], "row", row_peer(d)))
        g2[-1].start()

    for x in l1:
        x.wait_recv()
    mine = pl.ds(pl.multiple_of(r * lc, 8), lc)
    total = part_ref[mine]
    for d in range(1, nr):
        total += lbuf[d]
    left[mine] = total
    own = part_rows(left, r, lc)
    for d in range(1, nr):
        l2.append(send(own, own, l2s.at[d], l2r.at[d], "row", row_peer(d)))
        l2[-1].start()

    up, down = lax.rem(c + n, nc), lax.rem(c + nc - n, nc)
    origin = grp == r
    other = jnp.logical_not(origin)
    to_up = jnp.logical_and(grp >= r, grp + 1 < ng)
    to_down = jnp.logical_and(grp <= r, grp > 0)
    sends = []

    def hand_on(d, at_origin):
        chunk = lax.rem(r + nr - d, nr)
        there = part_rows(right, chunk, lc, lane * cal)
        u = send(there, there, cs.at[0, d], cr.at[d], "col", up)
        w = send(there, there, cs.at[1, d], cr.at[d], "col", down)
        near = [
            send(there, there, ss.at[e, d], sr.at[e, d], "col", grp * n + lax.rem(lane + e, n))
            for e in range(1, n)
        ]

        @pl.when(origin if at_origin else other)
        def _():
            if at_origin:
                if d > 0:
                    l2[d - 1].wait_recv()
                rows_in = pl.ds(pl.multiple_of(chunk * lc, 8), lc)
                rows_out = pl.ds(pl.multiple_of(lane * cal + chunk * lc, 8), lc)
                right[rows_out] = left[rows_in]
            else:
                u.wait_recv()
            pl.when(to_up)(u.start)
            pl.when(to_down)(w.start)
            for y in near:
                y.start()

        if not at_origin:
            sends.extend([(to_up, u), (to_down, w)] + [(None, y) for y in near])

    hand_on(0, True)
    for x in g2:
        x.wait_recv()
    total = gsum[...]
    for d in range(1, nr):
        total += gbuf2[d]
    gout[pl.ds(pl.multiple_of(c * ch, 8), ch)] = total
    gown = part_rows(gout, c, ch)
    for d in range(1, nc):
        g3.append(send(gown, gown, g3s.at[d], g3r.at[d], "col", col_peer(d)))
        g3[-1].start()
    for x in g3:
        x.wait_recv()

    work = small_work(gout, ainv, inv, x_out, sinv)
    next(work, None)
    hand_on(0, False)
    for d in range(1, nr):
        hand_on(d, True)
        next(work, None)
        hand_on(d, False)
        if d == nr // 2:
            for x in h1:
                x.wait_recv()
            mine = pl.ds(pl.multiple_of(r * hc, 8), hc)
            total = strip_ref[mine]
            for e in range(1, nr):
                total += hbuf[e]
            hm[mine] = total
            own = part_rows(hm, r, hc)
            for e in range(1, nr):
                h2.append(send(own, own, h2s.at[e], h2r.at[e], "row", row_peer(e)))
                h2[-1].start()
    for _ in work:
        pass

    for x in l2:
        pl.when(other)(x.wait_recv)
    for x in h2:
        x.wait_recv()
    for pred, x in sends:
        if pred is None:
            x.wait()
        else:
            pl.when(pred)(x.wait_send)
    for x in l1 + l2 + g1 + g2 + g3 + h1 + h2:
        x.wait_send()


def exchange(nr, nc, n, g, part, strip):
    f = jnp.float32
    dma = lambda *shape: pltpu.SemaphoreType.DMA(shape)
    cal, cols = part.shape
    ch = g.shape[0] // nc
    vmem = pl.BlockSpec(memory_space=pltpu.VMEM)
    return pl.pallas_call(
        functools.partial(exchange_kernel, nr, nc, n),
        in_specs=[vmem] * 3,
        out_specs=[vmem] * 8,
        out_shape=(
            jax.ShapeDtypeStruct(g.shape, f),
            jax.ShapeDtypeStruct(part.shape, f),
            jax.ShapeDtypeStruct((n * cal, cols), f),
            jax.ShapeDtypeStruct(strip.shape, f),
            jax.ShapeDtypeStruct((B, B), f),
            jax.ShapeDtypeStruct((cal, cal), f),
            jax.ShapeDtypeStruct((B, cal), f),
            jax.ShapeDtypeStruct((cal, cal), f),
        ),
        scratch_shapes=[
            pltpu.VMEM((nc, ch, g.shape[1]), f),
            pltpu.VMEM((ch, g.shape[1]), f),
            pltpu.VMEM((nr, ch, g.shape[1]), f),
            pltpu.VMEM((nr, cal // nr, cols), f),
            pltpu.VMEM((nr, B // nr, cols), f),
            dma(nc), dma(nc), dma(nr), dma(nr), dma(nc), dma(nc),
            dma(nr), dma(nr), dma(nr), dma(nr),
            dma(2, nr), dma(nr), dma(n, nr), dma(n, nr), dma(nr), dma(nr), dma(nr), dma(nr),
        ],
        compiler_params=pltpu.CompilerParams(
            collective_id=0, has_side_effects=True, vmem_limit_bytes=VMEM_LIMIT
        ),
        cost_estimate=pl.CostEstimate(
            flops=20 * cal * cols * B, bytes_accessed=64 * B * cols * 4, transcendentals=0
        ),
        name="exchange",
    )(g, part, strip)


def update_kernel(right_ref, inv_ref, left_ref, h_ref, out_ref, s_ref):
    cal = left_ref.shape[0]

    @pl.when(pl.program_id(0) == 0)
    def _():
        hi, lo = split2(dot(inv_ref[...], left_ref[...]))
        s_ref[0:cal] = hi
        s_ref[cal : 2 * cal] = lo
        s_ref[2 * cal : 3 * cal] = hi

    hi, lo = split2(right_ref[...].T)
    r = jnp.concatenate([hi, hi, lo], axis=1)
    out_ref[...] = h_ref[...] - bf_dot(r, s_ref[...])


def update_call(right, inv, left, h):
    cal = left.shape[0]
    rows, cols = h.shape
    t = tile_of(cols, 256)
    per = cols // t
    return pl.pallas_call(
        update_kernel,
        grid=(rows // t,),
        in_specs=[
            pl.BlockSpec((cal, t), lambda i: (i // per, i % per)),
            pl.BlockSpec(inv.shape, lambda i: (0, 0)),
            pl.BlockSpec(left.shape, lambda i: (0, 0)),
            pl.BlockSpec((t, cols), lambda i: (i, 0)),
        ],
        out_specs=pl.BlockSpec((t, cols), lambda i: (i, 0)),
        out_shape=jax.ShapeDtypeStruct(h.shape, jnp.float32),
        scratch_shapes=[pltpu.VMEM((3 * cal, cols), jnp.bfloat16)],
        compiler_params=params("arbitrary"),
        cost_estimate=pl.CostEstimate(
            flops=6 * cal * rows * cols, bytes_accessed=8 * rows * cols, transcendentals=0
        ),
        name="update",
    )(right, inv, left, h)


def prune_kernel(window_ref, comp_ref, w_ref, out_ref):
    product = bf_dot(window_ref[...], comp_ref[...])
    out_ref[...] = (w_ref[...].astype(jnp.float32) - product).astype(jnp.bfloat16)


def prune_call(window, comp, w):
    rows, cols = w.shape
    t = tile_of(rows, 512)
    return pl.pallas_call(
        prune_kernel,
        grid=(rows // t,),
        in_specs=[
            pl.BlockSpec((t, window.shape[1]), lambda i: (i, 0)),
            pl.BlockSpec(comp.shape, lambda i: (0, 0)),
            pl.BlockSpec((t, cols), lambda i: (i, 0)),
        ],
        out_specs=pl.BlockSpec((t, cols), lambda i: (i, 0)),
        out_shape=jax.ShapeDtypeStruct(w.shape, jnp.bfloat16),
        compiler_params=params("arbitrary"),
        cost_estimate=pl.CostEstimate(
            flops=2 * rows * cols * window.shape[1],
            bytes_accessed=4 * rows * cols,
            transcendentals=0,
        ),
        name="prune",
    )(window, comp, w)


def per_device(h, w, calib, block):
    rows, cols = h.shape
    r = lax.axis_index("row")
    c = lax.axis_index("col")
    start = block[0] * B
    owner_row, owner_col = start // rows, start // cols
    mine_row, mine_col = r == owner_row, c == owner_col
    off_row, off_col = start - owner_row * rows, start - owner_col * cols

    win = lax.dynamic_slice_in_dim(w, off_col, B, 1)
    win = jnp.where(mine_col, win, jnp.zeros_like(win))

    strip = lax.dynamic_slice_in_dim(h, off_row, B, 0)
    strip = jnp.where(mine_row, strip, 0.0)
    square = lax.dynamic_slice_in_dim(strip, off_col, B, 1)
    square = jnp.where(mine_col, square, 0.0)

    calib_rows = lax.dynamic_slice_in_dim(calib, r * rows, rows, 1)
    calib_cols = lax.dynamic_slice_in_dim(calib, c * cols, cols, 1).astype(jnp.float32)
    part = left_call(calib_rows, h)
    cal = part.shape[0]
    both = dot_t(jnp.concatenate([part, strip], axis=0), calib_cols)
    g = jnp.concatenate([both, square[:, :NB], square[:, NB:]], axis=0)

    g, win = lax.optimization_barrier((g, win))
    window = lax.psum(win, "col")

    g, left, right, hm, ainv, inv, x, sinv = exchange(
        lax.axis_size("row"), lax.axis_size("col"), rows // cols, g, part, strip
    )
    left, window = lax.optimization_barrier((left, window))
    comp = comp_call(hm, left, g[cal : cal + B], ainv, x, sinv)
    updated = update_call(right, inv, left, h)
    pruned = prune_call(window, comp, w)
    return (updated, pruned)


def solution(mesh):
    return jax.shard_map(
        per_device,
        mesh=mesh,
        in_specs=(P("row", "col"), P("row", "col"), P(), P()),
        out_specs=(P("row", "col"), P("row", "col")),
        check_vma=False,
    )
```

```python
import functools

import jax
import jax.numpy as jnp
from jax import lax
from jax.experimental import pallas as pl
from jax.experimental.pallas import tpu as pltpu
from jax.sharding import PartitionSpec as P

B = 256
NB = 128
STEP = 32
PIECES = 8
HIGH = lax.Precision.HIGHEST
VMEM_LIMIT = 48 * 1024 * 1024


def params(*semantics):
    return pltpu.CompilerParams(
        dimension_semantics=semantics or None, vmem_limit_bytes=VMEM_LIMIT
    )


def dot(a, b):
    return jnp.dot(a, b, precision=HIGH, preferred_element_type=jnp.float32)


def dot_t(a, b):
    return lax.dot_general(
        a, b, (((1,), (1,)), ((), ())), precision=HIGH, preferred_element_type=jnp.float32
    )


def bf_dot(a, b):
    return jnp.dot(a, b, preferred_element_type=jnp.float32)


def split2(x):
    hi = x.astype(jnp.bfloat16)
    lo = (x - hi.astype(jnp.float32)).astype(jnp.bfloat16)
    return hi, lo


def tile_of(n, most):
    t = most
    while n % t:
        t //= 2
    return t


def left_kernel(calib_ref, h_ref, out_ref):
    @pl.when(pl.program_id(0) == 0)
    def _():
        out_ref[...] = jnp.zeros_like(out_ref)

    c = calib_ref[...]
    hi, lo = split2(h_ref[...])
    out_ref[...] += bf_dot(c, hi) + bf_dot(c, lo)


def left_call(calib_rows, h):
    cal = calib_rows.shape[0]
    rows, cols = h.shape
    t = tile_of(rows, 512)
    return pl.pallas_call(
        left_kernel,
        grid=(rows // t,),
        in_specs=[
            pl.BlockSpec((cal, t), lambda i: (0, i)),
            pl.BlockSpec((t, cols), lambda i: (i, 0)),
        ],
        out_specs=pl.BlockSpec((cal, cols), lambda i: (0, 0)),
        out_shape=jax.ShapeDtypeStruct((cal, cols), jnp.float32),
        compiler_params=params("arbitrary"),
        cost_estimate=pl.CostEstimate(
            flops=4 * cal * rows * cols, bytes_accessed=4 * rows * cols, transcendentals=0
        ),
        name="left_part",
    )(calib_rows, h)


def inverses(mats, out):
    n = NB
    ri = lax.broadcasted_iota(jnp.int32, (n, n), 0)
    ci = lax.broadcasted_iota(jnp.int32, (n, n), 1)
    scales, ms = [], []
    for m in mats:
        only = jnp.where(ri == ci, m, 0.0)
        s_row = lax.rsqrt(jnp.sum(only, axis=0, keepdims=True))
        s_col = lax.rsqrt(jnp.sum(only, axis=1, keepdims=True))
        scales.append((s_row, s_col))
        ms.append(m * s_row * s_col)
    rk = lax.broadcasted_iota(jnp.int32, (n, 1), 0)
    ck = lax.broadcasted_iota(jnp.int32, (1, n), 1)
    for k in range(n):
        for i, m in enumerate(ms):
            row = m[k : k + 1, :]
            col = m[:, k : k + 1]
            inv = 1.0 / m[k : k + 1, k : k + 1]
            row = (row + jnp.where(ck == k, 1.0, 0.0)) * inv
            col = col - jnp.where(rk == k, 1.0, 0.0)
            ms[i] = m - col * row
        if k % STEP == STEP - 1:
            yield
    for m, (a, b) in zip(ms, scales):
        m = m * a * b
        out.append(0.5 * (m + m.T))


def small_work(g_ref, ainv_ref, inv_ref, x_ref, sinv_ref):
    n = NB
    cal = inv_ref.shape[0]
    inner = g_ref[0:cal]
    ri = lax.broadcasted_iota(jnp.int32, inner.shape, 0)
    ci = lax.broadcasted_iota(jnp.int32, inner.shape, 1)
    inner = jnp.where(ri == ci, 1.0, 0.0) + 0.5 * (inner + inner.T)
    base = cal + 2 * n
    a11 = g_ref[base : base + n]
    a21 = 0.5 * (g_ref[base + n : base + 2 * n] + g_ref[base + 2 * n : base + 3 * n].T)
    a22 = g_ref[base + 3 * n : base + 4 * n]
    out = []
    yield from inverses([0.5 * (a11 + a11.T)], out)
    p = out[0]
    w = dot(a21, p)
    q = 0.5 * (a22 + a22.T) - dot_t(w, a21)
    out = []
    yield from inverses([0.5 * (q + q.T), inner], out)
    q, inv = out
    inv_ref[...] = inv
    off = -dot(q, w)
    ainv_ref[:n, :n] = p - dot(w.T, off)
    ainv_ref[n:, :n] = off
    ainv_ref[:n, n:] = off.T
    ainv_ref[n:, n:] = q
    lmt = g_ref[cal:base]
    x = dot(ainv_ref[...], lmt)
    x_ref[...] = x
    sq = inner - dot(lmt.T, x)
    out = []
    yield from inverses([0.5 * (sq + sq.T)], out)
    sinv_ref[...] = out[0]


def comp_kernel(hm_ref, left_ref, lmt_ref, ainv_ref, x_ref, sinv_ref, out_ref):
    t = dot(ainv_ref[...], hm_ref[...])
    lm = lmt_ref[...].T
    v = dot(sinv_ref[...], left_ref[...] - dot(lm, t))
    out_ref[...] = (t - dot(x_ref[...], v)).astype(jnp.bfloat16)


def comp_call(hm, left, lmt, ainv, x, sinv):
    cols = hm.shape[1]
    t = tile_of(cols, 512)
    whole = lambda a: pl.BlockSpec(a.shape, lambda i: (0, 0))
    wide = lambda a: pl.BlockSpec((a.shape[0], t), lambda i: (0, i))
    return pl.pallas_call(
        comp_kernel,
        grid=(cols // t,),
        in_specs=[wide(hm), wide(left), whole(lmt), whole(ainv), whole(x), whole(sinv)],
        out_specs=pl.BlockSpec((hm.shape[0], t), lambda i: (0, i)),
        out_shape=jax.ShapeDtypeStruct(hm.shape, jnp.bfloat16),
        compiler_params=params("arbitrary"),
        name="comp",
    )(hm, left, lmt, ainv, x, sinv)


def exchange_kernel(
    nr, nc, n, g_ref, part_ref, strip_ref, win_ref, gout, left, right, hm, ainv, inv, x_out, sinv, wout,
    gbuf, gsum, gbuf2, lbuf, hbuf, wbuf, base, wu, wd, ru, rd,
    g1s, g1r, g2s, g2r, g3s, g3r, l1s, l1r, l2s, l2r, cs, cr, ss, sr, h1s, h1r, h2s, h2r,
    w0s, w0r, us, ur, ds, dr, w2s, w2r,
):
    r = lax.axis_index("row")
    c = lax.axis_index("col")
    grp, lane, ng = c // n, c % n, nc // n
    ch = g_ref.shape[0] // nc
    cal = part_ref.shape[0]
    lc = cal // nr
    hc = strip_ref.shape[0] // nr

    def send(src, dst, s, v, axis, peer):
        return pltpu.make_async_remote_copy(
            src_ref=src, dst_ref=dst, send_sem=s, recv_sem=v,
            device_id={axis: peer}, device_id_type=pl.DeviceIdType.MESH,
        )

    def row_peer(d):
        return lax.rem(r + d, nr)

    def col_peer(d):
        return lax.rem(c + d, nc)

    barrier = pltpu.get_barrier_semaphore()
    for d in range(1, nr):
        pl.semaphore_signal(
            barrier, inc=1, device_id={"row": row_peer(d)}, device_id_type=pl.DeviceIdType.MESH
        )
    for d in range(1, nc):
        pl.semaphore_signal(
            barrier, inc=1, device_id={"col": col_peer(d)}, device_id_type=pl.DeviceIdType.MESH
        )
    pl.semaphore_wait(barrier, nr + nc - 2)

    def part_rows(ref, i, size, base=0):
        return ref.at[pl.ds(pl.multiple_of(base + i * size, 8), size)]

    l1, l2, g1, g2, g3, h1, h2 = [], [], [], [], [], [], []
    for d in range(1, nr):
        p = row_peer(d)
        l1.append(send(part_rows(part_ref, p, lc), lbuf.at[d], l1s.at[d], l1r.at[d], "row", p))
        l1[-1].start()
    for d in range(1, nc):
        p = col_peer(d)
        g1.append(send(part_rows(g_ref, p, ch), gbuf.at[d], g1s.at[d], g1r.at[d], "col", p))
        g1[-1].start()
    for d in range(1, nr):
        p = row_peer(d)
        h1.append(send(part_rows(strip_ref, p, hc), hbuf.at[d], h1s.at[d], h1r.at[d], "row", p))
        h1[-1].start()

    wl = win_ref.shape[0] // n
    wq = wl // PIECES
    w0 = []
    for e in range(1, n):
        k = lax.rem(lane + e, n)
        w0.append(
            send(part_rows(win_ref, k, wl), wbuf.at[e], w0s.at[e], w0r.at[e], "col", grp * n + k)
        )
        w0[-1].start()
    has_up, has_down = grp + 1 < ng, grp > 0
    next_up, next_down = lax.rem(c + n, nc), lax.rem(c + nc - n, nc)
    wsends = []
    steps = PIECES + ng - 1

    def window_up(q):
        piece = pl.ds(pl.multiple_of(q * wq, 16), wq)
        return piece, send(wu.at[piece], ru.at[piece], us.at[q], ur.at[q], "col", next_up)

    def window_down(q):
        piece = pl.ds(pl.multiple_of(q * wq, 16), wq)
        return piece, send(wd.at[piece], rd.at[piece], ds.at[q], dr.at[q], "col", next_down)

    def pass_window(t):
        for q, make, out, came, has_in, has_out in (
            (t - grp, window_up, wu, ru, has_down, has_up),
            (t - (ng - 1 - grp), window_down, wd, rd, has_up, has_down),
        ):

            @pl.when(jnp.logical_and(q >= 0, q < PIECES))
            def _():
                piece, x = make(q)

                @pl.when(has_in)
                def _():
                    x.wait_recv()
                    out[piece] = base[piece] + came[piece]

                @pl.when(jnp.logical_not(has_in))
                def _():
                    out[piece] = base[piece]

                pl.when(has_out)(x.start)

    def finish_window():
        there = pl.ds(pl.multiple_of(lane * wl, 16), wl)

        @pl.when(has_down)
        def _():
            base[...] = base[...] + ru[...]

        @pl.when(has_up)
        def _():
            base[...] = base[...] + rd[...]

        wout[there] = base[...]
        for e in range(1, n):
            y = send(
                wout.at[there], wout.at[there], w2s.at[e], w2r.at[e], "col",
                grp * n + lax.rem(lane + e, n),
            )
            y.start()
            wsends.append((None, y))
        for q in range(PIECES):
            wsends.extend([(has_up, window_up(q)[1]), (has_down, window_down(q)[1])])

    for x in g1:
        x.wait_recv()
    total = g_ref[pl.ds(pl.multiple_of(c * ch, 8), ch)]
    for d in range(1, nc):
        total += gbuf[d]
    gsum[...] = total
    for d in range(1, nr):
        g2.append(send(gsum, gbuf2.at[d], g2s.at[d], g2r.at[d], "row", row_peer(d)))
        g2[-1].start()

    for x in l1:
        x.wait_recv()
    mine = pl.ds(pl.multiple_of(r * lc, 8), lc)
    total = part_ref[mine]
    for d in range(1, nr):
        total += lbuf[d]
    left[mine] = total
    own = part_rows(left, r, lc)
    for d in range(1, nr):
        l2.append(send(own, own, l2s.at[d], l2r.at[d], "row", row_peer(d)))
        l2[-1].start()

    up, down = lax.rem(c + n, nc), lax.rem(c + nc - n, nc)
    origin = grp == r
    other = jnp.logical_not(origin)
    to_up = jnp.logical_and(grp >= r, grp + 1 < ng)
    to_down = jnp.logical_and(grp <= r, grp > 0)
    sends = []

    def hand_on(d, at_origin):
        chunk = lax.rem(r + nr - d, nr)
        there = part_rows(right, chunk, lc, lane * cal)
        u = send(there, there, cs.at[0, d], cr.at[d], "col", up)
        w = send(there, there, cs.at[1, d], cr.at[d], "col", down)
        near = [
            send(there, there, ss.at[e, d], sr.at[e, d], "col", grp * n + lax.rem(lane + e, n))
            for e in range(1, n)
        ]

        @pl.when(origin if at_origin else other)
        def _():
            if at_origin:
                if d > 0:
                    l2[d - 1].wait_recv()
                rows_in = pl.ds(pl.multiple_of(chunk * lc, 8), lc)
                rows_out = pl.ds(pl.multiple_of(lane * cal + chunk * lc, 8), lc)
                right[rows_out] = left[rows_in]
            else:
                u.wait_recv()
            pl.when(to_up)(u.start)
            pl.when(to_down)(w.start)
            for y in near:
                y.start()

        if not at_origin:
            sends.extend([(to_up, u), (to_down, w)] + [(None, y) for y in near])

    hand_on(0, True)
    for x in g2:
        x.wait_recv()
    total = gsum[...]
    for d in range(1, nr):
        total += gbuf2[d]
    gout[pl.ds(pl.multiple_of(c * ch, 8), ch)] = total
    gown = part_rows(gout, c, ch)
    for d in range(1, nc):
        g3.append(send(gown, gown, g3s.at[d], g3r.at[d], "col", col_peer(d)))
        g3[-1].start()
    for x in w0:
        x.wait_recv()
    share = win_ref[pl.ds(pl.multiple_of(lane * wl, 16), wl)]
    for e in range(1, n):
        share += wbuf[e]
    base[...] = share
    pass_window(0)
    for x in g3:
        x.wait_recv()

    work = small_work(gout, ainv, inv, x_out, sinv)
    next(work, None)
    hand_on(0, False)
    passed = 1
    for d in range(1, nr):
        hand_on(d, True)
        next(work, None)
        hand_on(d, False)
        while passed < 1 + (steps - 1) * d // (nr - 1):
            next(work, None)
            pass_window(passed)
            passed += 1
        if d == nr // 2:
            for x in h1:
                x.wait_recv()
            mine = pl.ds(pl.multiple_of(r * hc, 8), hc)
            total = strip_ref[mine]
            for e in range(1, nr):
                total += hbuf[e]
            hm[mine] = total
            own = part_rows(hm, r, hc)
            for e in range(1, nr):
                h2.append(send(own, own, h2s.at[e], h2r.at[e], "row", row_peer(e)))
                h2[-1].start()
    finish_window()
    for _ in work:
        pass

    for x in l2:
        pl.when(other)(x.wait_recv)
    for x in h2:
        x.wait_recv()
    for pred, x in sends + wsends:
        if pred is None:
            x.wait()
        else:
            pl.when(pred)(x.wait_send)
    for x in l1 + l2 + g1 + g2 + g3 + h1 + h2 + w0:
        x.wait_send()


def exchange(nr, nc, n, g, part, strip, win):
    f = jnp.float32
    dma = lambda *shape: pltpu.SemaphoreType.DMA(shape)
    cal, cols = part.shape
    ch = g.shape[0] // nc
    wl = win.shape[0] // n
    vmem = pl.BlockSpec(memory_space=pltpu.VMEM)
    return pl.pallas_call(
        functools.partial(exchange_kernel, nr, nc, n),
        in_specs=[vmem] * 4,
        out_specs=[vmem] * 9,
        out_shape=(
            jax.ShapeDtypeStruct(g.shape, f),
            jax.ShapeDtypeStruct(part.shape, f),
            jax.ShapeDtypeStruct((n * cal, cols), f),
            jax.ShapeDtypeStruct(strip.shape, f),
            jax.ShapeDtypeStruct((B, B), f),
            jax.ShapeDtypeStruct((cal, cal), f),
            jax.ShapeDtypeStruct((B, cal), f),
            jax.ShapeDtypeStruct((cal, cal), f),
            jax.ShapeDtypeStruct(win.shape, win.dtype),
        ),
        scratch_shapes=[
            pltpu.VMEM((nc, ch, g.shape[1]), f),
            pltpu.VMEM((ch, g.shape[1]), f),
            pltpu.VMEM((nr, ch, g.shape[1]), f),
            pltpu.VMEM((nr, cal // nr, cols), f),
            pltpu.VMEM((nr, B // nr, cols), f),
            pltpu.VMEM((n, wl, win.shape[1]), win.dtype),
            *[pltpu.VMEM((wl, win.shape[1]), win.dtype)] * 5,
            dma(nc), dma(nc), dma(nr), dma(nr), dma(nc), dma(nc),
            dma(nr), dma(nr), dma(nr), dma(nr),
            dma(2, nr), dma(nr), dma(n, nr), dma(n, nr), dma(nr), dma(nr), dma(nr), dma(nr),
            dma(n), dma(n), *[dma(PIECES)] * 4, dma(n), dma(n),
        ],
        compiler_params=pltpu.CompilerParams(
            collective_id=0, has_side_effects=True, vmem_limit_bytes=VMEM_LIMIT
        ),
        cost_estimate=pl.CostEstimate(
            flops=20 * cal * cols * B, bytes_accessed=64 * B * cols * 4, transcendentals=0
        ),
        name="exchange",
    )(g, part, strip, win)


def update_kernel(right_ref, inv_ref, left_ref, h_ref, out_ref, s_ref):
    cal = left_ref.shape[0]

    @pl.when(pl.program_id(0) == 0)
    def _():
        hi, lo = split2(dot(inv_ref[...], left_ref[...]))
        s_ref[0:cal] = hi
        s_ref[cal : 2 * cal] = lo
        s_ref[2 * cal : 3 * cal] = hi

    hi, lo = split2(right_ref[...].T)
    r = jnp.concatenate([hi, hi, lo], axis=1)
    out_ref[...] = h_ref[...] - bf_dot(r, s_ref[...])


def update_call(right, inv, left, h):
    cal = left.shape[0]
    rows, cols = h.shape
    t = tile_of(cols, 768)
    per = cols // t
    return pl.pallas_call(
        update_kernel,
        grid=(rows // t,),
        in_specs=[
            pl.BlockSpec((cal, t), lambda i: (i // per, i % per)),
            pl.BlockSpec(inv.shape, lambda i: (0, 0)),
            pl.BlockSpec(left.shape, lambda i: (0, 0)),
            pl.BlockSpec((t, cols), lambda i: (i, 0)),
        ],
        out_specs=pl.BlockSpec((t, cols), lambda i: (i, 0)),
        out_shape=jax.ShapeDtypeStruct(h.shape, jnp.float32),
        scratch_shapes=[pltpu.VMEM((3 * cal, cols), jnp.bfloat16)],
        compiler_params=params("arbitrary"),
        cost_estimate=pl.CostEstimate(
            flops=6 * cal * rows * cols, bytes_accessed=8 * rows * cols, transcendentals=0
        ),
        name="update",
    )(right, inv, left, h)


def prune_kernel(window_ref, comp_ref, w_ref, out_ref):
    product = bf_dot(window_ref[...], comp_ref[...])
    out_ref[...] = (w_ref[...].astype(jnp.float32) - product).astype(jnp.bfloat16)


def prune_call(window, comp, w):
    rows, cols = w.shape
    t = tile_of(rows, 1536)
    return pl.pallas_call(
        prune_kernel,
        grid=(rows // t,),
        in_specs=[
            pl.BlockSpec((t, window.shape[1]), lambda i: (i, 0)),
            pl.BlockSpec(comp.shape, lambda i: (0, 0)),
            pl.BlockSpec((t, cols), lambda i: (i, 0)),
        ],
        out_specs=pl.BlockSpec((t, cols), lambda i: (i, 0)),
        out_shape=jax.ShapeDtypeStruct(w.shape, jnp.bfloat16),
        compiler_params=params("arbitrary"),
        cost_estimate=pl.CostEstimate(
            flops=2 * rows * cols * window.shape[1],
            bytes_accessed=4 * rows * cols,
            transcendentals=0,
        ),
        name="prune",
    )(window, comp, w)


def per_device(h, w, calib, block):
    rows, cols = h.shape
    r = lax.axis_index("row")
    c = lax.axis_index("col")
    start = block[0] * B
    owner_row, owner_col = start // rows, start // cols
    mine_row, mine_col = r == owner_row, c == owner_col
    off_row, off_col = start - owner_row * rows, start - owner_col * cols

    win = lax.dynamic_slice_in_dim(w, off_col, B, 1)
    win = jnp.where(mine_col, win, jnp.zeros_like(win))

    strip = lax.dynamic_slice_in_dim(h, off_row, B, 0)
    strip = jnp.where(mine_row, strip, 0.0)
    square = lax.dynamic_slice_in_dim(strip, off_col, B, 1)
    square = jnp.where(mine_col, square, 0.0)

    calib_rows = lax.dynamic_slice_in_dim(calib, r * rows, rows, 1)
    calib_cols = lax.dynamic_slice_in_dim(calib, c * cols, cols, 1).astype(jnp.float32)
    part = left_call(calib_rows, h)
    cal = part.shape[0]
    both = dot_t(jnp.concatenate([part, strip], axis=0), calib_cols)
    g = jnp.concatenate([both, square[:, :NB], square[:, NB:]], axis=0)

    g, left, right, hm, ainv, inv, x, sinv, window = exchange(
        lax.axis_size("row"), lax.axis_size("col"), rows // cols, g, part, strip, win
    )
    comp = comp_call(hm, left, g[cal : cal + B], ainv, x, sinv)
    updated = update_call(right, inv, left, h)
    pruned = prune_call(window, comp, w)
    return (updated, pruned)


def solution(mesh):
    return jax.shard_map(
        per_device,
        mesh=mesh,
        in_specs=(P("row", "col"), P("row", "col"), P(), P()),
        out_specs=(P("row", "col"), P("row", "col")),
        check_vma=False,
    )
```
